32 devices in a mesh: section: 2 (over core), seq: 4 (over z), head: 4 (over y, x).
Axes of the slice: x: 2, y: 2, z: 4, core: 2. Of those that a mesh axis runs over, the one named last changes fastest.
Arguments:
- hidden_in: float32 [4, 2048, 768], P(None, 'seq'), may hold values from -6 to 6
- out_grad: float32 [4, 2048, 768], P(None, 'seq'), may hold values from -6 to 6
- norm_gain: float32 [2, 768], P('section'), may hold values from 0.5 to 1.5
- input_weight: bfloat16 [2, 768, 2, 1536], P('section', None, None, 'head'), may hold values from -0.21875 to 0.21875
- bc_weight: bfloat16 [2, 768, 256], P('section'), may hold values from -0.21875 to 0.21875
- step_size_weight: bfloat16 [2, 768, 24], P('section', None, 'head'), may hold values from -0.21875 to 0.21875
- conv_inner: float32 [2, 4, 1536], P('section', None, 'head'), may hold values from -3 to 3
- conv_shared: float32 [2, 4, 256], P('section'), may hold values from -3 to 3
- bias_inner: float32 [2, 1536], P('section', 'head'), may hold values from -1.5 to 1.5
- bias_shared: float32 [2, 256], P('section'), may hold values from -1.5 to 1.5
- step_bias: float32 [2, 24], P('section', 'head'), may hold values from -5 to -3
- decay_log: float32 [2, 24], P('section', 'head'), may hold values from -6.5 to 0.5
- skip_gain: float32 [2, 24], P('section', 'head'), may hold values from 0.5 to 1.5
- inner_gain: float32 [2, 1536], P('section', 'head'), may hold values from 0.5 to 1.5
- output_weight: bfloat16 [2, 1536, 768], P('section', 'head'), may hold values from -0.15625 to 0.15625
Outputs:
- hidden_out: float32 [2, 4, 2048, 768], P('section', None, 'seq')
- input_grad: float32 [2, 4, 2048, 768], P('section', None, 'seq')
- norm_gain_grad: float32 [2, 768], P('section')
- proj_weight_grad: float32 [2, 768, 2, 1536], P('section', None, None, 'head')
- shared_weight_grad: float32 [2, 768, 256], P('section')
- step_weight_grad: float32 [2, 768, 24], P('section', None, 'head')
- conv_inner_grad: float32 [2, 4, 1536], P('section', None, 'head')
- conv_shared_grad: float32 [2, 4, 256], P('section')
- bias_inner_grad: float32 [2, 1536], P('section', 'head')
- bias_shared_grad: float32 [2, 256], P('section')
- step_bias_grad: float32 [2, 24], P('section', 'head')
- decay_log_grad: float32 [2, 24], P('section', 'head')
- skip_gain_grad: float32 [2, 24], P('section', 'head')
- inner_gain_grad: float32 [2, 1536], P('section', 'head')
- down_weight_grad: float32 [2, 1536, 768], P('section', 'head')
The draws below stay inside these ranges and needn't reach their ends.
All inputs are finite; a program needn't handle non-finite values.
Results may differ from the reference program's by a relative error of at most 0.014.
The reference program's roundings to bfloat16 on the way count: a program that leaves them out, or rounds other values in their place, can miss the bound.
Values sent between devices are 32-bit elements; how exact they have to be, the bound alone decides.
A program may use at most 256 MiB of HBM per device.

```python
import jax
import jax.numpy as jnp
from jax import lax

D = 768
DI = 1536
H = 24
N = 128
CONV = 4
SCAN_BLOCK = 256
LEN = 2048
SEQS = 4


def block_levels(stream_key, extent, shards, least, high):
    gain, own = 1.0, jax.random.fold_in(stream_key, 6)
    for dim, shards_of in shards:
        heights = jnp.exp(jax.random.uniform(jax.random.fold_in(own, dim), (shards_of,), jnp.float32, least / len(shards), high / len(shards)))
        gain = gain * jnp.repeat(heights, extent[dim] // shards_of).reshape([-1 if axis == dim else 1 for axis in range(len(extent))])
    return gain


def bell_draw(key, shape, scale, reach, cuts=(), dtype=jnp.bfloat16):
    loudness = block_levels(key, shape, cuts, -0.22, 0.18) if cuts else 1.0
    array = jax.random.normal(key, shape, jnp.float32) * scale * loudness
    return jnp.minimum(jnp.maximum(array, -reach), reach).astype(dtype)


def setup_inputs(seed: int = 0) -> dict:
    key_of = jax.random.split(jax.random.key(seed), 16)
    return {
        "hidden_in": bell_draw(key_of[0], (SEQS, LEN, D), 1.0, 6.0, ((1, 4),), jnp.float32),
        "out_grad": bell_draw(key_of[1], (SEQS, LEN, D), 1.0, 6.0, ((1, 4),), jnp.float32),
        "norm_gain": jnp.clip(1.0 + 0.1 * jax.random.normal(key_of[2], (2, D), jnp.float32), 0.5, 1.5),
        "input_weight": bell_draw(key_of[3], (2, D, 2, DI), D ** -0.5, 0.21875, ((0, 2), (3, 4))),
        "bc_weight": bell_draw(key_of[4], (2, D, 2 * N), D ** -0.5, 0.21875, ((0, 2),)),
        "step_size_weight": bell_draw(key_of[5], (2, D, H), D ** -0.5, 0.21875, ((0, 2), (2, 4))),
        "conv_inner": bell_draw(key_of[6], (2, CONV, DI), CONV ** -0.5, 3.0, ((0, 2), (2, 4)), jnp.float32),
        "conv_shared": bell_draw(key_of[7], (2, CONV, 2 * N), CONV ** -0.5, 3.0, ((0, 2),), jnp.float32),
        "bias_inner": bell_draw(key_of[8], (2, DI), 0.3, 1.5, ((0, 2), (1, 4)), jnp.float32),
        "bias_shared": bell_draw(key_of[9], (2, 2 * N), 0.3, 1.5, ((0, 2),), jnp.float32),
        "step_bias": jnp.clip(-5.0 + 2.0 * jax.random.uniform(key_of[10], (2, H), jnp.float32) ** block_levels(key_of[10], (2, H), ((0, 2), (1, 4)), -0.2, 0.2), -5.0, -3.0),
        "decay_log": jnp.clip(-6.5 + 7.0 * jax.random.uniform(key_of[11], (2, H), jnp.float32) ** block_levels(key_of[11], (2, H), ((0, 2), (1, 4)), -0.2, 0.2), -6.5, 0.5),
        "skip_gain": jnp.clip(0.5 + 1.0 * jax.random.uniform(key_of[12], (2, H), jnp.float32) ** block_levels(key_of[12], (2, H), ((0, 2), (1, 4)), -0.2, 0.2), 0.5, 1.5),
        "inner_gain": jnp.clip(1.0 + 0.1 * jax.random.normal(key_of[13], (2, DI), jnp.float32), 0.5, 1.5),
        "output_weight": bell_draw(key_of[14], (2, DI, D), DI ** -0.5, 0.15625, ((0, 2), (1, 4))),
    }


EPS = 1e-05
HIGHEST_PRECISION = lax.Precision.HIGHEST

@jax.custom_vjp
def low(v):
    return lax.optimization_barrier(v.astype(jnp.bfloat16)).astype(jnp.float32)

@jax.custom_vjp
def reduced_backward(v):
    return v

def low_keep(v):
    return (low(v), None)

def low_pass(kept, grad):
    return (grad,)

def back_keep(v):
    return (v, None)

def back_low(kept, grad):
    return (low(grad),)
low.defvjp(low_keep, low_pass)
reduced_backward.defvjp(back_keep, back_low)

def rms_scale(values):
    return values * lax.rsqrt(lax.optimization_barrier(jnp.mean(values * values, axis=-1, keepdims=True)) + EPS)

def conv_silu(padded, kernel, shift):
    length = padded.shape[1] - kernel.shape[0] + 1
    total = shift
    for offset in range(kernel.shape[0]):
        total = total + kernel[offset] * padded[:, offset:offset + length]
    return jax.nn.silu(total)

def block_terms(inner_x, b_mat, c_mat, step_size, rate):
    cumulative = jnp.cumsum(step_size * rate, axis=1)
    steps = inner_x.shape[1]
    lower = jnp.arange(steps)[:, None] >= jnp.arange(steps)[None, :]
    spread = cumulative[:, :, None, :] - cumulative[:, None, :, :]
    decays = jnp.exp(jnp.where(lower[None, :, :, None], spread, -1e+30))
    intersection = jnp.einsum('stn,sun->stu', c_mat, b_mat, precision=HIGHEST_PRECISION)
    mixing = intersection[..., None] * decays * step_size[:, None, :, :]
    y_intra = jnp.einsum('stuh,suhp->sthp', mixing, inner_x, precision=HIGHEST_PRECISION)
    tail = jnp.exp(cumulative[:, -1:, :] - cumulative) * step_size
    state = jnp.einsum('suh,suhp,sun->shpn', tail, inner_x, b_mat, precision=HIGHEST_PRECISION)
    return (y_intra, state, cumulative)

def carried(c_mat, cumulative, start):
    return jnp.exp(cumulative)[..., None] * jnp.einsum('stn,shpn->sthp', c_mat, start, precision=HIGHEST_PRECISION)

def layer(hidden, norm_gain, input_weight, bc_weight, step_size_weight, conv_inner, conv_shared, bias_inner, bias_shared, step_bias, decay_log, skip_gain, inner_gain, output_weight):
    seqs, length, width = hidden.shape
    inner_width = input_weight.shape[2]
    heads = decay_log.shape[0]
    head_size = inner_width // heads
    normalized_input = low(rms_scale(hidden) * norm_gain)
    gate_logits = reduced_backward(jnp.einsum('nzt,tv->nzv', normalized_input, input_weight[:, 0], precision=HIGHEST_PRECISION))
    projected_mixer_input = reduced_backward(jnp.einsum('nzt,tv->nzv', normalized_input, input_weight[:, 1], precision=HIGHEST_PRECISION))
    step_logits = reduced_backward(jnp.einsum('nzt,tv->nzv', normalized_input, step_size_weight, precision=HIGHEST_PRECISION))
    projected_bc_values = jnp.einsum('nzt,tv->nzv', normalized_input, bc_weight, precision=HIGHEST_PRECISION)
    mixed_in = jnp.concatenate([projected_mixer_input, projected_bc_values], axis=-1)
    padded = jnp.pad(mixed_in, ((0, 0), (CONV - 1, 0), (0, 0)))
    conv_out = conv_silu(padded, jnp.concatenate([conv_inner, conv_shared], axis=1), jnp.concatenate([bias_inner, bias_shared]))
    inner_x = conv_out[..., :inner_width].reshape(seqs, length, heads, head_size)
    b_mat = conv_out[..., inner_width:inner_width + N]
    c_mat = conv_out[..., inner_width + N:]
    step_size = jax.nn.softplus(step_logits + step_bias)
    rate = -jnp.exp(decay_log)
    blocks = length // SCAN_BLOCK

    def cut(values):
        return jnp.moveaxis(values.reshape((seqs, blocks, SCAN_BLOCK) + values.shape[2:]), 1, 0)

    def block_step(start, pieces):
        x_block, b_block, c_block, s_block = pieces
        y_intra, state, cumulative = block_terms(x_block, b_block, c_block, s_block, rate)
        y_block = y_intra + carried(c_block, cumulative, start)
        new_start = jnp.exp(cumulative[:, -1])[..., None, None] * start + state
        return (new_start, y_block)
    start_zero = jnp.zeros((seqs, heads, head_size, N), jnp.float32)
    _, y_blocks = lax.scan(jax.checkpoint(block_step), start_zero, (cut(inner_x), cut(b_mat), cut(c_mat), cut(step_size)))
    mixed_out = jnp.moveaxis(y_blocks, 0, 1).reshape(seqs, length, heads, head_size) + skip_gain[:, None] * inner_x
    mixed_out = mixed_out.reshape(seqs, length, inner_width)
    gated = mixed_out * jax.nn.silu(gate_logits)
    normalized_output = low(rms_scale(gated) * inner_gain)
    branch_output = reduced_backward(jnp.einsum('bzv,vw->bzw', normalized_output, output_weight, precision=HIGHEST_PRECISION))
    return hidden + branch_output

def reference(hidden_in, out_grad, norm_gain, input_weight, bc_weight, step_size_weight, conv_inner, conv_shared, bias_inner, bias_shared, step_bias, decay_log, skip_gain, inner_gain, output_weight):
    params = [value.astype(jnp.float32) for value in (norm_gain, input_weight, bc_weight, step_size_weight, conv_inner, conv_shared, bias_inner, bias_shared, step_bias, decay_log, skip_gain, inner_gain, output_weight)]
    first = [value[0] for value in params]
    second = [value[1] for value in params]
    middle, first_vjp = jax.vjp(layer, hidden_in.astype(jnp.float32), *first)
    final, second_vjp = jax.vjp(layer, middle, *second)
    second_grads = second_vjp(out_grad.astype(jnp.float32))
    first_grads = first_vjp(second_grads[0])
    stacked = [jnp.stack([first_grads[index], second_grads[index]]) for index in range(14)]
    return (stacked_pair(middle, final), stacked[0], stacked[1], stacked[2], stacked[3], stacked[4], stacked[5], stacked[6], stacked[7], stacked[8], stacked[9], stacked[10], stacked[11], stacked[12], stacked[13])

def stacked_pair(first_value, second_value):
    return jnp.stack([first_value, second_value])
```

```python
import jax
import jax.numpy as jnp
from jax import lax
from jax.sharding import PartitionSpec as P

DI = 1536
P_SIZE = 64
N = 128
CONV = 4
SCAN_BLOCK = 256


EPS = 1e-05
HIGHEST_PRECISION = lax.Precision.HIGHEST
HIGH_PRECISION = lax.Precision.HIGH


def running_sum(values):
    steps = values.shape[1]
    lower = (jnp.arange(steps)[:, None] >= jnp.arange(steps)[None, :]).astype(jnp.float32)
    return jnp.einsum("ts,gsh->gth", lower, values, precision=HIGHEST_PRECISION)


def between(log_decays, reverse):
    count = lax.axis_size("seq")
    place = lax.axis_index("seq")
    sources = jnp.arange(count)
    if reverse:
        inside = (sources[None, :] > place) & (sources[None, :] < sources[:, None])
        valid = sources > place
    else:
        inside = (sources[None, :] < place) & (sources[None, :] > sources[:, None])
        valid = sources < place
    log_sum = jnp.sum(
        jnp.where(inside[:, :, None, None], log_decays[None], 0.0), axis=1
    )
    return jnp.where(valid[:, None, None], jnp.exp(log_sum), 0.0)


def swapped(x):
    return lax.ppermute(x, "section", [(0, 1), (1, 0)])


def passed_along(x, axis, by):
    length = lax.axis_size(axis)
    pairs = [(i, i + by) for i in range(length) if 0 <= i + by < length]
    return lax.ppermute(x, axis, pairs)


def traded(x, axis, bit):
    count = lax.axis_size(axis)
    return lax.ppermute(x, axis, [(i, i ^ bit) for i in range(count)])


def head_sum(x):
    count = lax.axis_size("head")
    rows = x.shape[0]
    if count != 4 or rows % 8:
        return lax.psum(x, "head")
    place = lax.axis_index("head")
    parts = x.reshape(2, 4, rows // 8, x.shape[1])
    sums = []
    for part, bits in ((0, (1, 2)), (1, (2, 1))):
        value = parts[part].reshape(2, 2, rows // 8, x.shape[1])
        upper = [(place & bit) != 0 for bit in bits]
        keep = jnp.where(upper[0], value[1], value[0])
        give = jnp.where(upper[0], value[0], value[1])
        value = keep + traded(give, "head", bits[0])
        keep = jnp.where(upper[1], value[1], value[0])
        give = jnp.where(upper[1], value[0], value[1])
        sums.append([keep + traded(give, "head", bits[1]), upper, bits])
    out = []
    for value, upper, bits in sums:
        came = traded(value, "head", bits[1])
        value = jnp.where(
            upper[1], jnp.concatenate([came, value]), jnp.concatenate([value, came])
        )
        came = traded(value, "head", bits[0])
        out.append(
            jnp.where(upper[0], jnp.concatenate([came, value]), jnp.concatenate([value, came]))
        )
    return jnp.concatenate(out)


def norm_piece(hidden, gain):
    return hidden * lax.rsqrt(jnp.mean(hidden * hidden, axis=-1, keepdims=True) + EPS) * gain


def conv_silu(padded, kernel, shift):
    length = padded.shape[1] - kernel.shape[0] + 1
    total = shift
    for offset in range(kernel.shape[0]):
        total = total + kernel[offset] * padded[:, offset : offset + length]
    return jax.nn.silu(total)


def block_terms(inner_x, b_mat, c_mat, step_size, rate):
    cumulative = running_sum(step_size * rate)
    steps = inner_x.shape[1]
    lower = jnp.arange(steps)[:, None] >= jnp.arange(steps)[None, :]
    spread = cumulative[:, :, None, :] - cumulative[:, None, :, :]
    decays = jnp.exp(jnp.where(lower[None, :, :, None], spread, -1e30))
    intersection = jnp.einsum("stn,sun->stu", c_mat, b_mat, precision=HIGH_PRECISION)
    mixing = intersection[..., None] * decays * step_size[:, None, :, :]
    y_intra = jnp.einsum("stuh,suhp->sthp", mixing, inner_x, precision=HIGH_PRECISION)
    tail = jnp.exp(cumulative[:, -1:, :] - cumulative) * step_size
    state = jnp.einsum("suh,suhp,sun->shpn", tail, inner_x, b_mat, precision=HIGH_PRECISION)
    return (y_intra, state, cumulative)


def carried(c_mat, cumulative, start):
    return jnp.exp(cumulative)[..., None] * jnp.einsum(
        "stn,shpn->sthp", c_mat, start, precision=HIGH_PRECISION
    )


def mixer_front(extended, step_logits, kernel, shift, step_bias, decay_log, skip_gain):
    group, padded_len, channels = extended.shape
    steps_dev = padded_len - CONV + 1
    heads_local = decay_log.shape[0]
    inner_local = heads_local * P_SIZE
    conv_out = conv_silu(extended, kernel, shift)
    inner_x = conv_out[..., :inner_local].reshape(group, steps_dev, heads_local, P_SIZE)
    b_mat = conv_out[..., inner_local : inner_local + N]
    c_mat = conv_out[..., inner_local + N :]
    step_size = jax.nn.softplus(step_logits + step_bias)
    rate = -jnp.exp(decay_log)
    block = min(SCAN_BLOCK, steps_dev)
    blocks = steps_dev // block

    def cut(values):
        return jnp.moveaxis(values.reshape((group, blocks, block) + values.shape[2:]), 1, 0)

    def block_step(start, pieces):
        x_block, b_block, c_block, s_block = pieces
        y_intra, state, block_cum = block_terms(x_block, b_block, c_block, s_block, rate)
        y_block = y_intra + carried(c_block, block_cum, start)
        new_start = jnp.exp(block_cum[:, -1])[..., None, None] * start + state
        return (new_start, y_block)

    start_zero = jnp.zeros((group, heads_local, P_SIZE, N), jnp.float32)
    final_state, y_blocks = lax.scan(
        jax.checkpoint(block_step),
        start_zero,
        (cut(inner_x), cut(b_mat), cut(c_mat), cut(step_size)),
    )
    y_local = jnp.moveaxis(y_blocks, 0, 1).reshape(group, steps_dev, heads_local, P_SIZE)
    cumulative = running_sum(step_size * rate)
    return (
        y_local + skip_gain[:, None] * inner_x,
        final_state,
        cumulative[:, -1],
        cumulative,
        c_mat,
    )


def pass_states(state, log_decay):
    group, heads, size, width = state.shape
    row = jnp.broadcast_to(log_decay[:, :, None, None], (group, heads, 1, width))
    gathered = lax.all_gather(jnp.concatenate([state, row], axis=2), "seq")
    log_decays = gathered[:, :, :, size, 0]
    weight = between(log_decays, False)
    return (jnp.sum(weight[..., None, None] * gathered[:, :, :, :size], axis=0), log_decays)


def pass_grads(start_grad, log_decays):
    grads = lax.all_gather(start_grad, "seq")
    weight = between(log_decays, True)
    return jnp.sum(weight[..., None, None] * grads, axis=0)


def rows_product(left, right):
    return lax.dot_general(
        left, right, (((0,), (0,)), ((), ())), preferred_element_type=jnp.float32
    )


def layer_forward(current, weights):
    gain, w_main, w_shared, kernel, shift, step_bias, decay_log, skip_gain, inner_gain, w_down = (
        weights
    )
    group, steps_dev, width = current.shape
    inner_local = inner_gain.shape[0]
    heads_local = decay_log.shape[0]
    normalized_input, norm_vjp = jax.vjp(norm_piece, current, gain)
    flat_rows = normalized_input.astype(jnp.bfloat16).reshape(group * steps_dev, width)
    main_proj = jnp.dot(flat_rows, w_main, preferred_element_type=jnp.float32)
    shared_proj = jnp.dot(flat_rows, w_shared, preferred_element_type=jnp.float32)
    gate_logits = main_proj[:, :inner_local].reshape(group, steps_dev, inner_local)
    projected_mixer_input = main_proj[:, inner_local : 2 * inner_local]
    step_logits = main_proj[:, 2 * inner_local :].reshape(group, steps_dev, heads_local)
    mixed_in = jnp.concatenate([projected_mixer_input, shared_proj], axis=1).reshape(
        group, steps_dev, -1
    )
    rim_rows = mixed_in[:, steps_dev - (CONV - 1) :]
    before = passed_along(rim_rows, "seq", 1)
    extended = jnp.concatenate([before, mixed_in], axis=1)
    front, front_vjp = jax.vjp(
        mixer_front, extended, step_logits, kernel, shift, step_bias, decay_log, skip_gain
    )
    y_local, state, log_decay, cumulative, c_mat = front
    start, kept_decay = pass_states(state, log_decay)
    y_carry, carry_vjp = jax.vjp(carried, c_mat, cumulative, start)
    mixed_out = (y_local + y_carry).reshape(group, steps_dev, inner_local)
    gated = mixed_out * jax.nn.silu(gate_logits)
    total = lax.psum(jnp.sum(gated * gated, axis=-1), "head")
    rstd = lax.rsqrt(total / DI + EPS)[..., None]
    normalized_output = (
        (gated * rstd * inner_gain).astype(jnp.bfloat16).reshape(group * steps_dev, inner_local)
    )
    partial_value = jnp.dot(normalized_output, w_down, preferred_element_type=jnp.float32)
    branch_output = head_sum(partial_value)
    result = current + branch_output.reshape(group, steps_dev, width)
    kept = (
        flat_rows,
        norm_vjp,
        gate_logits,
        mixed_out,
        gated,
        rstd,
        normalized_output,
        front_vjp,
        carry_vjp,
        start,
        log_decay,
        kept_decay,
    )
    return (result, kept)


def layer_backward(cotangent, kept, weights, pending):
    gain, w_main, w_shared, kernel, shift, step_bias, decay_log, skip_gain, inner_gain, w_down = (
        weights
    )
    (
        flat_rows,
        norm_vjp,
        gate_logits,
        mixed_out,
        gated,
        rstd,
        normalized_output,
        front_vjp,
        carry_vjp,
        start,
        log_decay,
        kept_decay,
    ) = kept
    group, steps_dev, width = cotangent.shape
    inner_local = inner_gain.shape[0]
    heads_local = decay_log.shape[0]
    down_grad = cotangent.astype(jnp.bfloat16).reshape(group * steps_dev, width)
    d_down = rows_product(normalized_output, down_grad)
    d_normed = lax.dot_general(
        down_grad, w_down, (((1,), (1,)), ((), ())), preferred_element_type=jnp.float32
    )
    d_normed = d_normed.reshape(group, steps_dev, inner_local)
    d_inner_gain = jnp.sum(d_normed * gated * rstd, axis=(0, 1))
    scaled_grad = d_normed * inner_gain
    dot_total = lax.psum(jnp.sum(scaled_grad * gated, axis=-1), "head")
    d_gated = rstd * scaled_grad - gated * rstd * rstd * rstd * dot_total[..., None] / DI
    sigmoid_gate = jax.nn.sigmoid(gate_logits)
    d_mixed = (d_gated * gate_logits * sigmoid_gate).reshape(group, steps_dev, heads_local, P_SIZE)
    d_gate = d_gated * mixed_out * sigmoid_gate * (1.0 + gate_logits * (1.0 - sigmoid_gate))
    d_cmat, d_cumulative, d_start = carry_vjp(d_mixed)
    state_grad, pending = lax.optimization_barrier((pass_grads(d_start, kept_decay), pending))
    d_log = jnp.exp(log_decay) * jnp.sum(state_grad * start, axis=(2, 3))
    d_ext, d_dt, d_kernel, d_shift, d_bias_step, d_decay, d_skip = front_vjp(
        (d_mixed, state_grad, d_log, d_cumulative, d_cmat)
    )
    back_rows = passed_along(d_ext[:, : CONV - 1], "seq", -1)
    d_in_mix = d_ext[:, CONV - 1 :] + jnp.pad(
        back_rows, ((0, 0), (steps_dev - CONV + 1, 0), (0, 0))
    )
    rows = group * steps_dev
    d_main = jnp.concatenate(
        [
            d_gate.reshape(rows, inner_local),
            d_in_mix[..., :inner_local].reshape(rows, inner_local),
            d_dt.reshape(rows, heads_local),
        ],
        axis=1,
    ).astype(jnp.bfloat16)
    d_shared = d_in_mix[..., inner_local:].reshape(rows, 2 * N)
    d_main_w = rows_product(flat_rows, d_main)
    d_shared_w = lax.dot_general(
        flat_rows,
        d_shared.astype(jnp.bfloat16),
        (((0,), (0,)), ((), ())),
        preferred_element_type=jnp.float32,
    )
    d_normed_in = lax.dot_general(
        d_main, w_main, (((1,), (1,)), ((), ())), preferred_element_type=jnp.float32
    )
    d_normed_in = d_normed_in + lax.dot_general(
        d_shared.astype(jnp.bfloat16),
        w_shared,
        (((1,), (1,)), ((), ())),
        preferred_element_type=jnp.float32,
    )
    d_hidden, d_gain = norm_vjp(d_normed_in.reshape(group, steps_dev, width))
    input_total = cotangent + head_sum(d_hidden.reshape(group * steps_dev, width)).reshape(
        group, steps_dev, width
    )
    grads = (
        d_gain,
        d_main_w,
        d_shared_w,
        d_kernel,
        d_shift,
        d_bias_step,
        d_decay,
        d_skip,
        d_inner_gain,
        d_down,
    )
    return (input_total, grads, pending)


def joined(values):
    return jnp.concatenate([value.reshape(-1) for value in values])


def stacked(flat, width):
    rows = -(-flat.shape[0] // (8 * width)) * 8
    return jnp.pad(flat, (0, rows * width - flat.shape[0])).reshape(rows, width)


def total_terms(terms):
    main_half, down_wide, shared_wide = terms
    return lax.psum((main_half, down_wide, lax.psum(shared_wide, "head")), "seq")


def parted(flat, likes):
    out = []
    at = 0
    for like in likes:
        out.append(flat[at : at + like.size].reshape(like.shape))
        at += like.size
    return out


def shards(
    hidden_in,
    out_grad,
    norm_gain,
    input_weight,
    bc_weight,
    step_size_weight,
    conv_inner,
    conv_shared,
    bias_inner,
    bias_shared,
    step_bias,
    decay_log,
    skip_gain,
    inner_gain,
    output_weight,
):
    section = lax.axis_index("section")
    first = section == 0
    seqs_all, steps_dev, width = hidden_in.shape
    inner_local = inner_gain.shape[1]
    mine = seqs_all // 2
    w_main = jnp.concatenate(
        [input_weight[0].reshape(width, 2 * inner_local), step_size_weight[0]], axis=1
    )
    kernel = jnp.concatenate([conv_inner[0], conv_shared[0]], axis=1)
    shift = jnp.concatenate([bias_inner[0], bias_shared[0]])
    own = (
        norm_gain[0],
        w_main,
        bc_weight[0],
        kernel,
        shift,
        step_bias[0],
        decay_log[0],
        skip_gain[0],
        inner_gain[0],
        output_weight[0],
    )
    here = first.astype(jnp.float32)
    layers = ([], [])
    for value in own:
        mine32 = value.astype(jnp.float32)
        other = swapped(mine32)
        layers[0].append((mine32 * here + other * (1.0 - here)).astype(value.dtype))
        layers[1].append((other * here + mine32 * (1.0 - here)).astype(value.dtype))
    current = lax.dynamic_slice_in_dim(hidden_in, section * mine, mine, 0)
    saved = []
    hidden = []
    for weights in layers:
        current, kept = layer_forward(current, weights)
        saved.append(kept)
        hidden.append(current)
    cotangent = lax.dynamic_slice_in_dim(out_grad, section * mine, mine, 0)

    def whole(pair):
        keep = jnp.where(first, pair[0], pair[1])
        came = swapped(jnp.where(first, pair[1], pair[0]))
        return jnp.where(
            first, jnp.concatenate([keep, came]), jnp.concatenate([came, keep])
        )

    hidden_all = whole(hidden)
    inputs = [None, None]
    summed = [None, None]
    pending = ()
    for layer in (1, 0):
        cotangent, grads, pending = layer_backward(
            cotangent, saved[layer], layers[layer], pending
        )
        inputs[layer] = cotangent
        d_gain, d_main, d_shared, d_kernel, d_shift, d_bias, d_decay, d_skip, d_inner, d_down = grads
        if layer == 1:
            cotangent, hidden_all = lax.optimization_barrier((cotangent, hidden_all))
        halved = []
        for value in (d_main, d_down, d_shared):
            rows = value.shape[0] // 2
            low, high = value[:rows], value[rows:]
            halved.append(jnp.where(first, low, high) + swapped(jnp.where(first, high, low)))
        small = joined([d_kernel[:, :inner_local], d_shift[:inner_local], d_bias, d_decay, d_skip, d_inner])
        common = joined([d_gain, d_kernel[:, inner_local:], d_shift[inner_local:]])
        common = common + swapped(common)
        small = small + swapped(small)
        shared_wide = jnp.concatenate([halved[2], stacked(common, halved[2].shape[1])])
        down_wide = jnp.concatenate([halved[1], stacked(small, width)])
        terms = (halved[0], down_wide, shared_wide)
        if layer == 1:
            pending = terms
            continue
        main_half, down_wide, shared_wide = lax.psum(pending, "seq")
        summed[1] = (main_half, down_wide, lax.psum(shared_wide, "head"))
        terms, summed[1] = lax.optimization_barrier((terms, summed[1]))
        summed[0] = total_terms(terms)
    shared_rows = halved[2].shape[0]
    down_rows = halved[1].shape[0]
    summed = [
        (
            main_half,
            down_wide[:down_rows],
            shared_wide[:shared_rows],
            down_wide[down_rows:].reshape(-1),
            shared_wide[shared_rows:].reshape(-1),
        )
        for main_half, down_wide, shared_wide in summed
    ]
    grads_all = whole(inputs)
    main_sum, down_sum, shared_sum = [
        whole([summed[0][place], summed[1][place]]) for place in range(3)
    ]
    small, common = [jnp.where(first, summed[0][place], summed[1][place]) for place in (3, 4)]
    kernel_inner, shift_inner, bias_step_sum, decay_sum, skip_sum, inner_sum = parted(
        small,
        [conv_inner[0], bias_inner[0], step_bias[0], decay_log[0], skip_gain[0], inner_gain[0]],
    )
    gain_sum, kernel_shared, shift_shared = parted(
        common, [norm_gain[0], conv_shared[0], bias_shared[0]]
    )
    proj_grad = main_sum[:, : 2 * inner_local].reshape(width, 2, inner_local)
    step_grad = main_sum[:, 2 * inner_local :]
    return (
        hidden_all[None],
        grads_all[None],
        gain_sum[None],
        proj_grad[None],
        shared_sum[None],
        step_grad[None],
        kernel_inner[None],
        kernel_shared[None],
        shift_inner[None],
        shift_shared[None],
        bias_step_sum[None],
        decay_sum[None],
        skip_sum[None],
        inner_sum[None],
        down_sum[None],
    )


def solution(mesh):
    in_specs = (
        P(None, "seq", None),
        P(None, "seq", None),
        P("section", None),
        P("section", None, None, "head"),
        P("section", None, None),
        P("section", None, "head"),
        P("section", None, "head"),
        P("section", None, None),
        P("section", "head"),
        P("section", None),
        P("section", "head"),
        P("section", "head"),
        P("section", "head"),
        P("section", "head"),
        P("section", "head", None),
    )
    out_specs = (
        P("section", None, "seq", None),
        P("section", None, "seq", None),
        P("section", None),
        P("section", None, None, "head"),
        P("section", None, None),
        P("section", None, "head"),
        P("section", None, "head"),
        P("section", None, None),
        P("section", "head"),
        P("section", None),
        P("section", "head"),
        P("section", "head"),
        P("section", "head"),
        P("section", "head"),
        P("section", "head", None),
    )
    return jax.shard_map(shards, mesh=mesh, in_specs=in_specs, out_specs=out_specs, check_vma=False)
```
